128 devices in a mesh: row: 8 (over y, core), col: 16 (over x, z).
Axes of the slice: x: 4, y: 4, z: 4, core: 2. Of those that a mesh axis runs over, the one named last changes fastest.
Arguments:
- features: bfloat16 [32768, 128], P(('row', 'col')), may hold values from -6 to 6
- tile_values: bfloat16 [8, 16, 512, 128, 128], P('row', 'col'), may hold values from -0.03125 to 0.03125
- tile_coords: int32 [8, 16, 2, 512], P('row', 'col'), may hold values from 0 to 31, as said below
- tile_count: int32 [8, 16], P('row', 'col'), may hold values from 128 to 512, as said below
- weight: bfloat16 [128, 256], replicated, may hold values from -0.5 to 0.5
- bias: float32 [256], replicated, may hold values from -3 to 3
- cotangent: bfloat16 [32768, 256], P(('row', 'col')), may hold values from -6 to 6
Outputs:
- layer_out: bfloat16 [32768, 256], P(('row', 'col'))
- weight_grad: float32 [128, 256], replicated
- bias_grad: float32 [256], replicated
- feature_grad: float32 [32768, 128], P(('row', 'col'))
The draws below stay inside these ranges and needn't reach their ends.
Inputs may be any that keep to these rules, and one draw needn't show every extreme that they name: `tile_coords`: each device's tile row entries lie below 32 and tile column entries below 16, in every slot; some device has a tile row 31. `tile_count`: some device has all 512 slots live.
All inputs are finite; a program needn't handle non-finite values.
Results may differ from the reference program's by a relative error of at most 0.007.
Values may be sent and summed in bfloat16 or wider, within the bound.
A program may use at most 192 MiB of HBM per device.

```python
import jax
import jax.numpy as jnp
from jax import lax

F = 128
HID = 256
BLK = 128
ROWS_DEV = 256
TILES = 512
NODES = 32768
ROW_BLOCKS = 32
COL_BLOCKS = 16
N_ROW = 8
N_COL = 16


def draw_tile_coords(key, part):
    key = jax.random.fold_in(key, 2)
    keys = jax.random.split(key, 7)
    per_block = ROWS_DEV // BLK
    shape = (N_ROW, N_COL, TILES)
    row_ids = jnp.arange(N_ROW, dtype=jnp.int32).reshape(N_ROW, 1, 1)
    col_ids = jnp.arange(N_COL, dtype=jnp.int32).reshape(1, N_COL, 1)
    within = jax.random.randint(keys[0], shape, 0, per_block, dtype=jnp.int32)
    spread = jax.random.randint(keys[1], shape, -per_block, 2 * per_block, dtype=jnp.int32)
    near_rows = (col_ids * per_block + spread + ROW_BLOCKS) % ROW_BLOCKS
    near_cols = jnp.broadcast_to(row_ids * per_block + within, shape)
    far_pick = jax.random.randint(keys[2], (N_ROW, N_COL, 4), 0, COL_BLOCKS, dtype=jnp.int32)
    which_far = jax.random.randint(keys[3], shape, 0, 4, dtype=jnp.int32)
    far_cols = jnp.take_along_axis(far_pick, which_far, axis=2)
    far_rows = jax.random.randint(keys[4], shape, 0, ROW_BLOCKS, dtype=jnp.int32)
    is_far = jax.random.randint(keys[5], shape, 0, 10, dtype=jnp.int32) < 3
    tile_rows = jnp.where(is_far, far_rows, near_rows).astype(jnp.int32)
    tile_cols = jnp.where(is_far, far_cols, near_cols).astype(jnp.int32)
    chosen = jax.random.randint(keys[6], (2,), 0, 1 << 20, dtype=jnp.int32)
    tile_rows = tile_rows.at[chosen[0] % N_ROW, chosen[1] % N_COL, 0].set(ROW_BLOCKS - 1)
    return jnp.stack([tile_rows, tile_cols], axis=2)


def draw_tile_count(key, part):
    key = jax.random.fold_in(key, 7)
    key_level, key_pick = jax.random.split(key)
    levels = jax.random.randint(key_level, (N_ROW * N_COL,), 0, 3, dtype=jnp.int32)
    divisor = jnp.array([1, 2, 4], dtype=jnp.int32)[levels]
    counts = jnp.maximum(TILES // divisor, 1)
    chosen = jax.random.randint(key_pick, (), 0, N_ROW * N_COL, dtype=jnp.int32)
    counts = counts.at[chosen].set(TILES)
    return counts.reshape(N_ROW, N_COL).astype(jnp.int32)


def shard_levels(stream_key, dims, shards, least, largest):
    def one(dim, parts):
        draws = jax.random.uniform(jax.random.fold_in(jax.random.fold_in(stream_key, 6), dim), (parts,), jnp.float32, least / len(shards), largest / len(shards))
        return jnp.repeat(jnp.exp(draws), dims[dim] // parts).reshape((-1,) + (1,) * (len(dims) - dim - 1))

    factor_of = one(*shards[0])
    for cut in shards[1:]:
        factor_of = factor_of * one(*cut)
    return factor_of


def normal_values(rng, shape, deviation, limit, cuts=(), kind=jnp.bfloat16):
    drawn = deviation * jax.random.normal(rng, shape, jnp.float32)
    if cuts:
        drawn = drawn * shard_levels(rng, shape, cuts, -0.22, 0.18)
    return jnp.clip(drawn, -limit, limit).astype(kind)


def setup_inputs(seed: int = 0) -> dict:
    arg_keys = jax.random.split(jax.random.key(seed), 8)
    return {
        "features": normal_values(arg_keys[0], (NODES, F), 1.0, 6.0, ((0, 128),)),
        "tile_values": normal_values(arg_keys[1], (N_ROW, N_COL, TILES, BLK, BLK), (TILES * BLK * N_COL // ROW_BLOCKS) ** -0.5, 0.03125, ((0, 8), (1, 16))),
        "tile_coords": draw_tile_coords(jax.random.fold_in(arg_keys[7], 71), 0),
        "tile_count": draw_tile_count(jax.random.fold_in(arg_keys[7], 71), 0),
        "weight": normal_values(arg_keys[4], (F, HID), F ** -0.5, 0.5),
        "bias": normal_values(arg_keys[5], (HID,), 0.5, 3.0, (), jnp.float32),
        "cotangent": normal_values(arg_keys[6], (NODES, HID), 1.0, 6.0, ((0, 128),)),
    }


def tile_products(values, out_index, in_index, tile_total, source, segments, transposed):
    feat_width = source.shape[1]
    blocks = source.reshape(-1, values.shape[1], feat_width)
    picked = blocks[in_index].astype(jnp.float32)
    tiles = values.astype(jnp.float32)
    if transposed:
        products = jnp.einsum('tji,tjf->tif', tiles, picked, precision=lax.Precision.HIGHEST)
    else:
        products = jnp.einsum('tij,tjf->tif', tiles, picked, precision=lax.Precision.HIGHEST)
    alive_mask = jnp.arange(values.shape[0], dtype=jnp.int32) < tile_total
    target = jnp.where(alive_mask, out_index, segments).astype(jnp.int32)
    summed = jax.ops.segment_sum(products, target, num_segments=segments)
    return summed.reshape(segments * values.shape[1], feat_width)

def reference(features, tile_values, tile_coords, tile_count, weight, bias, cotangent):
    by_device = features.reshape(N_ROW, N_COL, ROWS_DEV, F)

    def row_group(rindex):

        def add_device(total, cindex):
            column_feats = by_device[:, cindex].reshape(N_ROW * ROWS_DEV, F)
            coords = tile_coords[rindex, cindex]
            term = tile_products(tile_values[rindex, cindex], coords[0], coords[1], tile_count[rindex, cindex], column_feats, ROW_BLOCKS, False)
            return (total + term, None)
        total, unused = lax.scan(add_device, jnp.zeros((ROW_BLOCKS * BLK, F), jnp.float32), jnp.arange(N_COL, dtype=jnp.int32))
        return total
    aggregated = lax.map(row_group, jnp.arange(N_ROW, dtype=jnp.int32)).reshape(NODES, F)
    agg_bf = aggregated.astype(jnp.bfloat16)
    pre = jnp.dot(agg_bf, weight, preferred_element_type=jnp.float32) + bias
    layer_out = (pre * jax.nn.sigmoid(pre)).astype(jnp.bfloat16)
    sigma = jax.nn.sigmoid(pre)
    slope_grad = (cotangent.astype(jnp.float32) * sigma * (1.0 + pre * (1.0 - sigma))).astype(jnp.bfloat16)
    scale_factor = 1.0 / jnp.sqrt(jnp.float32(NODES))
    weight_grad = jnp.dot(agg_bf.T, slope_grad, preferred_element_type=jnp.float32) * scale_factor
    bias_grad = lax.optimization_barrier(jnp.sum(slope_grad.astype(jnp.float32), axis=0)) * scale_factor
    vertex_grad = jnp.dot(slope_grad, weight.T, preferred_element_type=jnp.float32).astype(jnp.bfloat16)
    by_group = vertex_grad.reshape(N_ROW, N_COL * ROWS_DEV, F)

    def column_group(cindex):

        def add_device(total, rindex):
            coords = tile_coords[rindex, cindex]
            term = tile_products(tile_values[rindex, cindex], coords[1], coords[0], tile_count[rindex, cindex], by_group[rindex], COL_BLOCKS, True)
            return (total + term, None)
        total, unused = lax.scan(add_device, jnp.zeros((COL_BLOCKS * BLK, F), jnp.float32), jnp.arange(N_ROW, dtype=jnp.int32))
        return total
    columns = lax.map(column_group, jnp.arange(N_COL, dtype=jnp.int32)).reshape(N_COL, N_ROW, ROWS_DEV, F)
    feature_grad = jnp.transpose(columns, (1, 0, 2, 3)).reshape(NODES, F)
    return (layer_out, weight_grad, bias_grad, feature_grad)
```

```python
import functools
import math

import jax
import jax.numpy as jnp
from jax import lax
from jax.experimental import pallas as pl
from jax.experimental.pallas import tpu as pltpu
from jax.sharding import PartitionSpec as P

f32, bf16, i32 = jnp.float32, jnp.bfloat16, jnp.int32
MESH = pl.DeviceIdType.MESH
BLK = 128
LOADS = 8


def kernel(
    feats_hbm, tiles_hbm, coords_hbm, count_ref, weight_hbm, bias_ref, cot_hbm,
    out_ref, wgrad_ref, bgrad_ref, fgrad_ref,
    raw, slots, xg, coords, weight, cot, meta_v, meta,
    part, recv_a, recv_b, sum_a, sum_b, recv_a2, recv_b2,
    grads, back, rs1_out, rs1_in, rs2_out, rs2_in,
    w1, w2, w3, w4, w5, w6,
    load_sem, send_sem, recv_sem,
):
    tiles = raw.shape[0]
    row, col = lax.axis_index("row"), lax.axis_index("col")
    y, core = lax.div(row, 2), lax.rem(row, 2)
    x, z = lax.div(col, 4), lax.rem(col, 4)

    def device(dy=0, dcore=0, dx=0, dz=0):
        return (
            lax.rem(y + dy, 4) * 2 + lax.rem(core + dcore, 2),
            lax.rem(x + dx, 4) * 4 + lax.rem(z + dz, 4),
        )

    counter = [0]

    def remote(src, dst, sem, **where):
        return pltpu.make_async_remote_copy(
            src_ref=src,
            dst_ref=dst,
            send_sem=send_sem.at[sem],
            recv_sem=recv_sem.at[sem],
            device_id=device(**where),
            device_id_type=MESH,
        )

    def take(count):
        first = counter[0]
        counter[0] += count
        return first

    sent = []

    def send(*args, **where):
        copy = remote(*args, **where)
        copy.start()
        sent.append(copy)
        return copy

    barrier = pltpu.get_barrier_semaphore()
    peers = [device(dcore=1)]
    for d in (1, 2, 3):
        peers += [device(dy=d), device(dx=d), device(dz=d)]
    for peer in peers:
        pl.semaphore_signal(barrier, inc=1, device_id=peer, device_id_type=MESH)

    def load(src, dst, sem):
        copy = pltpu.make_async_copy(src, dst, load_sem.at[sem])
        copy.start()
        return copy

    coords_load = load(coords_hbm.at[0, 0], coords, 0)
    feats_load = load(feats_hbm, xg.at[row], 1)
    step = tiles // LOADS
    tile_loads = [
        load(
            tiles_hbm.at[0, 0, pl.ds(n * step, step)],
            raw.at[pl.ds(n * step, step)],
            4 + n,
        )
        for n in range(LOADS)
    ]
    weight_load = load(weight_hbm, weight, 2)
    cot_load = load(cot_hbm, cot, 3)

    slots[tiles] = jnp.zeros((BLK, BLK), bf16)
    coords_load.wait()
    lanes = lax.broadcasted_iota(i32, (1, tiles), 1)
    live = lanes < count_ref[0, 0]
    pos = jnp.where(live, coords[0:1, :] * 16 + coords[1:2, :], tiles)
    key = pos * tiles + lanes

    def down(v):
        return jnp.transpose(jnp.broadcast_to(v, (BLK, tiles)))

    def count(mask):
        return jnp.sum(jnp.where(mask, 1, 0), axis=0, keepdims=True)

    pos_down, key_down = down(pos), down(key)
    rank, first = [], []
    for n in range(tiles // BLK):
        cut = slice(n * BLK, (n + 1) * BLK)
        before = key_down < key[:, cut]
        rank.append(count(before))
        first.append(count(before & (pos_down == pos[:, cut])))
    rank = jnp.concatenate(rank, axis=1)
    first = jnp.concatenate(first, axis=1)
    code = lanes * 2 + jnp.where(first == 0, 1, 0)
    rank_down, code_down = down(rank), down(code)
    for n in range(tiles // BLK):
        cut = slice(n * BLK, (n + 1) * BLK)
        at = lanes[:, cut]
        meta_v[0:1, cut] = jnp.sum(jnp.where(rank_down == at, code_down, 0), axis=0, keepdims=True)
        upto, here = count(pos_down <= at), count(pos_down == at)
        meta_v[1:2, cut] = jnp.where(here == 0, tiles, upto - 1)
    meta_load = load(meta_v, meta, 0)

    pl.semaphore_wait(barrier, len(peers))
    feats_load.wait()
    sem = take(3)
    near = [send(xg.at[row], xg.at[row], sem + d - 1, dy=d) for d in (1, 2, 3)]
    side_sem = take(4)
    side = [send(xg.at[row], xg.at[row], side_sem, dcore=1)]
    meta_load.wait()
    for copy in tile_loads:
        copy.wait()

    unroll = 16
    quarter = tiles // 4

    def compress(base, acc):
        def some(i, acc):
            for u in range(unroll):
                k = base + i * unroll + u
                c = meta[0, k]
                value = raw[lax.shift_right_logical(c, 1)].astype(f32)
                acc = jnp.where((c & 1) == 1, value, acc + value)
                slots[k] = acc.astype(bf16)
            return acc

        return lax.fori_loop(0, quarter // unroll, some, acc)

    acc = jnp.zeros((BLK, BLK), f32)
    for n in range(4):
        acc = compress(n * quarter, acc)
        if n == 2:
            for d in (1, 2, 3):
                near[d - 1].wait_recv()
                other = lax.rem(y + 4 - d, 4) * 2 + core
                side.append(send(xg.at[other], xg.at[other], side_sem + d, dcore=1))
    for copy in side:
        copy.wait_recv()

    sem_a, sem_b = take(3), take(12)

    def a_copy(q, xq):
        return remote(part.at[xq, 0], recv_a.at[q], sem_a + q, dx=q + 1)

    def b_copy(q, xq, d):
        return remote(
            part.at[xq, 1, lax.rem(z + d, 4)], recv_b.at[d - 1, xq], sem_b + q * 3 + d - 1, dz=d
        )

    def tile(r, c):
        return slots[meta[1, r * 16 + c]]

    def forward(q, carry):
        xq = lax.rem(x + 1 + q, 4)
        lhs = jnp.concatenate(
            [
                jnp.concatenate([tile(2 * (4 * xq + zz) + h, c) for c in range(16)], axis=1)
                for h in range(2)
                for zz in range(4)
            ],
            axis=0,
        )
        source = xg[...].reshape(16 * BLK, BLK)
        product = jnp.dot(lhs, source, preferred_element_type=f32)
        part[xq] = product.astype(bf16).reshape(2, 4, BLK, BLK)

        @pl.when(q < 3)
        def _():
            a_copy(q, xq).start()

        for d in (1, 2, 3):
            b_copy(q, xq, d).start()
        return carry

    lax.fori_loop(0, 4, forward, 0)
    xqs = [lax.rem(x + 1 + q, 4) for q in range(4)]
    for q in range(4):
        if q < 3:
            sent.append(a_copy(q, xqs[q]))
        for d in (1, 2, 3):
            sent.append(b_copy(q, xqs[q], d))

    second_a, second_b = take(3), take(3)
    got_a, got_b = [], []

    def b_sum(q):
        total = part[xqs[q], 1, z].astype(f32)
        for d in (1, 2, 3):
            b_copy(q, xqs[q], d).wait_recv()
            total = total + recv_b[d - 1, xqs[q]].astype(f32)
        return total

    for q in range(3):
        sum_b[q] = b_sum(q).astype(bf16)
        got_b.append(send(sum_b.at[q], recv_b2.at[q], second_b + q, dx=q + 1))
    total = part[x, 0].astype(f32)
    for q in range(3):
        a_copy(q, xqs[q]).wait_recv()
        total = total + recv_a[q].astype(f32)
    sum_a[...] = total.astype(bf16)
    for d in (1, 2, 3):
        got_a.append(send(sum_a.at[lax.rem(z + d, 4)], recv_a2.at[d - 1], second_a + d - 1, dz=d))
    half_b = b_sum(3)
    half_a = sum_a[z].astype(f32)
    for q in range(3):
        got_b[q].wait_recv()
        half_b = half_b + recv_b2[q].astype(f32)
    for q in range(3):
        got_a[q].wait_recv()
        half_a = half_a + recv_a2[q].astype(f32)
    aggregated = jnp.concatenate([half_a, half_b], axis=0)
    agg = aggregated.astype(bf16)

    weight_load.wait()
    cot_load.wait()
    pre = jnp.dot(agg, weight[...], preferred_element_type=f32) + bias_ref[...]
    sigma = jax.nn.sigmoid(pre)
    slope = (cot[...].astype(f32) * sigma * (1.0 + pre * (1.0 - sigma))).astype(bf16)
    vertex = lax.dot_general(
        weight[...], slope, (((1,), (1,)), ((), ())), preferred_element_type=f32
    ).astype(bf16)
    grads[col, 0] = vertex[:, :BLK]
    grads[col, 1] = vertex[:, BLK:]

    sem_ax, sem_bz, sem_az, sem_bx = take(3), take(3), take(3), take(3)
    sem_af, sem_bf = take(9), take(9)
    own_a, own_b = grads.at[col, 0], grads.at[col, 1]
    ax = [send(own_a, own_a, sem_ax + d - 1, dx=d) for d in (1, 2, 3)]
    bz = [send(own_b, own_b, sem_bz + d - 1, dz=d) for d in (1, 2, 3)]
    az = [send(own_a, own_a, sem_az + d - 1, dz=d) for d in (1, 2, 3)]
    bx = [send(own_b, own_b, sem_bx + d - 1, dx=d) for d in (1, 2, 3)]

    out_ref[...] = (pre * sigma).astype(bf16)
    wide = slope.astype(f32)
    bias_part = wide[0:8]
    for n in range(1, wide.shape[0] // 8):
        bias_part = bias_part + wide[n * 8 : n * 8 + 8]
    weight_part = jnp.dot(
        jnp.transpose(agg.astype(f32)).astype(bf16), slope, preferred_element_type=f32
    )

    w_sem1, w_sem2, w_sem3, w_sem4, w_sem5, w_sem6 = (take(n) for n in (3, 3, 1, 3, 3, 3))
    for n in range(4):
        w1[n, 0, 0:32] = weight_part[n * 32 : n * 32 + 32]
        w1[n, 0, 32:40] = bias_part

    def w1_start():
        return [
            send(w1.at[lax.rem(x + d, 4), 0], w1.at[0, d], w_sem1 + d - 1, dx=d)
            for d in (1, 2, 3)
        ]

    def in_order(me, own, received):
        total = None
        for n in range(4):
            term = own
            for d in (1, 2, 3):
                term = jnp.where(lax.rem(me + 4 - d, 4) == n, received[d - 1], term)
            total = term if total is None else total + term
        return total

    w_got1 = w1_start()

    af, bf = {}, {}
    for e in (1, 2, 3):
        ax[e - 1].wait_recv()
        from_x = grads.at[lax.rem(x + 4 - e, 4) * 4 + z, 0]
        for d in (1, 2, 3):
            af[e, d] = send(from_x, from_x, sem_af + (e - 1) * 3 + d - 1, dz=d)
        bz[e - 1].wait_recv()
        from_z = grads.at[x * 4 + lax.rem(z + 4 - e, 4), 1]
        for d in (1, 2, 3):
            bf[e, d] = send(from_z, from_z, sem_bf + (e - 1) * 3 + d - 1, dx=d)

    def group(g):
        zg, xg_ = lax.rem(z + 4 - g, 4), lax.rem(x + 4 - g, 4)
        return [(xx * 4 + zg, 0) for xx in range(4)] + [(xg_ * 4 + zz, 1) for zz in range(4)]

    def backward(g, i):
        members = group(g)
        lhs = jnp.concatenate([grads[j, h] for j, h in members], axis=1)
        rhs = jnp.concatenate(
            [
                jnp.concatenate([tile(2 * j + h, 2 * i + b) for b in range(2)], axis=1)
                for j, h in members
            ],
            axis=0,
        )
        return jnp.dot(lhs, rhs, preferred_element_type=f32)

    def first_group(i, carry):
        back[i] = backward(0, i)
        return carry

    lax.fori_loop(0, 8, first_group, 0)

    for copy in w_got1:
        copy.wait_recv()
    total = in_order(x, w1[x, 0], [w1[0, d] for d in (1, 2, 3)])
    for n in range(4):
        w2[n, 0, 0:8] = total[n * 8 : n * 8 + 8]
        w2[n, 0, 8:16] = total[32:40]
    w_got2 = [
        send(w2.at[lax.rem(z + d, 4), 0], w2.at[0, d], w_sem2 + d - 1, dz=d) for d in (1, 2, 3)
    ]

    def arrive(g):
        az[g - 1].wait_recv()
        bx[g - 1].wait_recv()
        for e in (1, 2, 3):
            af[e, g].wait_recv()
            bf[e, g].wait_recv()

    def add_group(g):
        arrive(g)

        def one(i, carry):
            back[i] += backward(g, i)
            return carry

        lax.fori_loop(0, 8, one, 0)

    add_group(1)

    for copy in w_got2:
        copy.wait_recv()
    w3[0] = in_order(z, w2[z, 0], [w2[0, d] for d in (1, 2, 3)])
    w_got3 = send(w3.at[0], w3.at[1], w_sem3, dcore=1)

    add_group(2)

    w_got3.wait_recv()
    w4[0] = w3[0] + w3[1]
    w_got4 = [send(w4.at[0], w4.at[d], w_sem4 + d - 1, dy=d) for d in (1, 2, 3)]

    arrive(3)
    rs_sem1, rs_sem2 = take(4), take(3)
    order = (1, 2, 3, 0)
    got1 = []
    for n, d in enumerate(order):
        r = lax.rem(y + d, 4) * 2 + (1 - core)
        rs1_out[n] = (back[r] + backward(3, r)).astype(bf16)
        got1.append(send(rs1_out.at[n], rs1_in.at[n], rs_sem1 + n, dcore=1))
    got2 = []
    for n, d in enumerate(order):
        r = lax.rem(y + d, 4) * 2 + core
        total = back[r] + backward(3, r)
        got1[n].wait_recv()
        total = total + rs1_in[n].astype(f32)
        if d:
            rs2_out[n] = total.astype(bf16)
            got2.append(send(rs2_out.at[n], rs2_in.at[n], rs_sem2 + n, dy=d))

    for copy in w_got4:
        copy.wait_recv()
    summed = in_order(y, w4[0], [w4[d] for d in (1, 2, 3)])
    scale = 1.0 / math.sqrt(256 * lax.axis_size("row") * lax.axis_size("col"))
    w5[z] = summed[0:8] * scale
    w_got5 = [send(w5.at[z], w5.at[z], w_sem5 + d - 1, dz=d) for d in (1, 2, 3)]
    bgrad_ref[...] = jnp.sum(summed[8:16], axis=0, keepdims=True) * scale
    for copy in w_got5:
        copy.wait_recv()
    w6[x] = w5[...].reshape(32, 256)
    w_got6 = [send(w6.at[x], w6.at[x], w_sem6 + d - 1, dx=d) for d in (1, 2, 3)]

    for n in range(3):
        got2[n].wait_recv()
        total = total + rs2_in[n].astype(f32)
    fgrad_ref[...] = jnp.transpose(total)
    for copy in w_got6:
        copy.wait_recv()
    wgrad_ref[...] = w6[...].reshape(128, 256)
    for copy in sent:
        copy.wait_send()
    assert counter[0] <= SEMS, counter[0]


SEMS = 96


def local(features, tile_values, tile_coords, tile_count, weight, bias, cotangent):
    tiles = tile_values.shape[2]
    vmem = pl.BlockSpec(memory_space=pltpu.VMEM)
    smem = pl.BlockSpec(memory_space=pltpu.SMEM)
    anywhere = pl.BlockSpec(memory_space=pl.ANY)
    square = (BLK, BLK)
    out, wgrad, bgrad, fgrad = pl.pallas_call(
        kernel,
        name="graph_layer",
        out_shape=(
            jax.ShapeDtypeStruct((256, 256), bf16),
            jax.ShapeDtypeStruct((128, 256), f32),
            jax.ShapeDtypeStruct((1, 256), f32),
            jax.ShapeDtypeStruct((256, 128), f32),
        ),
        in_specs=[anywhere, anywhere, anywhere, smem, anywhere, vmem, anywhere],
        out_specs=(vmem, vmem, vmem, vmem),
        scratch_shapes=[
            pltpu.VMEM((tiles, *square), bf16),
            pltpu.VMEM((tiles + 1, *square), bf16),
            pltpu.VMEM((8, 256, 128), bf16),
            pltpu.VMEM((2, tiles), i32),
            pltpu.VMEM((128, 256), bf16),
            pltpu.VMEM((256, 256), bf16),
            pltpu.VMEM((2, tiles), i32),
            pltpu.SMEM((2, tiles), i32),
            pltpu.VMEM((4, 2, 4, *square), bf16),
            pltpu.VMEM((3, 4, *square), bf16),
            pltpu.VMEM((3, 4, *square), bf16),
            pltpu.VMEM((4, *square), bf16),
            pltpu.VMEM((3, *square), bf16),
            pltpu.VMEM((3, *square), bf16),
            pltpu.VMEM((3, *square), bf16),
            pltpu.VMEM((16, 2, *square), bf16),
            pltpu.VMEM((8, 128, 256), f32),
            pltpu.VMEM((4, 128, 256), bf16),
            pltpu.VMEM((4, 128, 256), bf16),
            pltpu.VMEM((3, 128, 256), bf16),
            pltpu.VMEM((3, 128, 256), bf16),
            pltpu.VMEM((4, 4, 40, 256), f32),
            pltpu.VMEM((4, 4, 16, 256), f32),
            pltpu.VMEM((2, 16, 256), f32),
            pltpu.VMEM((4, 16, 256), f32),
            pltpu.VMEM((4, 8, 256), f32),
            pltpu.VMEM((4, 32, 256), f32),
            pltpu.SemaphoreType.DMA((4 + LOADS,)),
            pltpu.SemaphoreType.DMA((SEMS,)),
            pltpu.SemaphoreType.DMA((SEMS,)),
        ],
        compiler_params=pltpu.CompilerParams(
            collective_id=0, has_side_effects=True, vmem_limit_bytes=56 * 2**20
        ),
    )(features, tile_values, tile_coords, tile_count, weight, bias.reshape(1, 256), cotangent)
    return out, wgrad, bgrad.reshape(256), fgrad


def solution(mesh):
    placed = (
        P(("row", "col"), None),
        P("row", "col", None, None, None),
        P("row", "col", None, None),
        P("row", "col"),
        P(),
        P(),
        P(("row", "col"), None),
    )
    return jax.shard_map(
        local,
        mesh=mesh,
        in_specs=placed,
        out_specs=(P(("row", "col"), None), P(), P(), P(("row", "col"), None)),
        check_vma=False,
    )
```

```python
import functools
import math

import jax
import jax.numpy as jnp
from jax import lax
from jax.experimental import pallas as pl
from jax.experimental.pallas import tpu as pltpu
from jax.sharding import PartitionSpec as P

f32, bf16, i32 = jnp.float32, jnp.bfloat16, jnp.int32
MESH = pl.DeviceIdType.MESH
BLK = 128


def kernel(
    feats_hbm, tiles_hbm, coords_hbm, count_hbm, weight_hbm, bias_hbm, cot_hbm,
    out_ref, wgrad_ref, bgrad_ref, fgrad_ref,
    raw0, raw1, slots, seeds, xg, coords, alive, weight, bias, cot, meta_v, meta,
    part, recv_a, recv_b, sum_a, sum_b, recv_a2, recv_b2,
    grads, back, rs1_out, rs1_in, rs2_out, rs2_in,
    w1, w2, w3, w4, w5,
    load_sem, send_sem, recv_sem,
):
    raws = (raw0, raw1)
    tiles = 2 * raw0.shape[0]
    row, col = lax.axis_index("row"), lax.axis_index("col")
    y, core = lax.div(row, 2), lax.rem(row, 2)
    x, z = lax.div(col, 4), lax.rem(col, 4)

    def device(dy=0, dcore=0, dx=0, dz=0):
        return (
            lax.rem(y + dy, 4) * 2 + lax.rem(core + dcore, 2),
            lax.rem(x + dx, 4) * 4 + lax.rem(z + dz, 4),
        )

    counter = [0]

    def remote(src, dst, sem, **where):
        return pltpu.make_async_remote_copy(
            src_ref=src,
            dst_ref=dst,
            send_sem=send_sem.at[sem],
            recv_sem=recv_sem.at[sem],
            device_id=device(**where),
            device_id_type=MESH,
        )

    def take(count):
        first = counter[0]
        counter[0] += count
        return first

    sent = []

    def send(*args, **where):
        copy = remote(*args, **where)
        copy.start()
        sent.append(copy)
        return copy

    def load(src, dst, sem):
        copy = pltpu.make_async_copy(src, dst, load_sem.at[sem])
        copy.start()
        return copy

    half = tiles // 2
    coords_load = load(coords_hbm.at[0, 0], coords, 0)
    count_load = load(count_hbm, alive, 1)
    feats_load = load(feats_hbm, xg.at[row], 2)
    tile_loads = [
        load(tiles_hbm.at[0, 0, pl.ds(n * half, half)], raws[n], 3 + n)
        for n in range(2)
    ]
    weight_load = load(weight_hbm, weight, 5)
    bias_load = load(bias_hbm, bias, 6)
    cot_load = load(cot_hbm, cot, 7)

    barrier = pltpu.get_barrier_semaphore()
    peers = [device(dcore=1)]
    for d in (1, 2, 3):
        peers += [device(dy=d), device(dx=d), device(dz=d)]
    for peer in peers:
        pl.semaphore_signal(barrier, inc=1, device_id=peer, device_id_type=MESH)

    slots[tiles] = jnp.zeros((BLK, BLK), bf16)
    seeds[half] = jnp.zeros((BLK, BLK), bf16)
    coords_load.wait()
    count_load.wait()
    lanes = lax.broadcasted_iota(i32, (1, tiles), 1)
    pos = jnp.where(lanes < alive[...], coords[0:1, :] * 16 + coords[1:2, :], tiles)

    def down(v):
        return jnp.transpose(jnp.broadcast_to(v, (BLK, v.shape[1])))

    def count(mask):
        return jnp.sum(jnp.where(mask, 1, 0), axis=0, keepdims=True)

    key = pos * tiles + lanes
    ranks, firsts = [], []
    pos_down, key_down = down(pos), down(key)
    for n in range(tiles // BLK):
        cut = slice(n * BLK, (n + 1) * BLK)
        same = slice(0, half) if n < tiles // BLK // 2 else slice(half, tiles)
        before = key_down[same] < key[:, cut]
        ranks.append(count(before))
        firsts.append(count(before & (pos_down[same] == pos[:, cut])))

    pl.semaphore_wait(barrier, len(peers))
    feats_load.wait()
    sem = take(3)
    near = [send(xg.at[row], xg.at[row], sem + d - 1, dy=d) for d in (1, 2, 3)]
    side_sem = take(4)
    side = [send(xg.at[row], xg.at[row], side_sem, dcore=1)]

    rank = jnp.concatenate(ranks, axis=1)
    first = jnp.where(jnp.concatenate(firsts, axis=1) == 0, 1, 0)
    seed = []
    for n in range(tiles // BLK):
        cut = slice(n * BLK, (n + 1) * BLK)
        if n < tiles // BLK // 2:
            seed.append(jnp.full((1, BLK), half, i32))
        else:
            upto, here = count(pos_down[:half] <= pos[:, cut]), count(pos_down[:half] == pos[:, cut])
            seed.append(jnp.where(here == 0, half, upto - 1))
    code = (jnp.concatenate(seed, axis=1) * tiles + lanes) * 2 + first
    rank_down, code_down = down(rank), down(code)
    for n in range(tiles // BLK):
        cut = slice(n * BLK, (n + 1) * BLK)
        at = lanes[:, cut]
        same = slice(0, half) if n < tiles // BLK // 2 else slice(half, tiles)
        slot = at if n < tiles // BLK // 2 else at - half
        meta_v[0:1, cut] = jnp.sum(
            jnp.where(rank_down[same] == slot, code_down[same], 0), axis=0, keepdims=True
        )
        upto0, here0 = count(pos_down[:half] <= at), count(pos_down[:half] == at)
        upto1, here1 = count(pos_down[half:] <= at), count(pos_down[half:] == at)
        early = jnp.where(here0 == 0, tiles, upto0 - 1)
        meta_v[1:2, cut] = jnp.where(here1 == 0, early, half + upto1 - 1)
    meta_load = load(meta_v, meta, 0)
    meta_load.wait()

    unroll = 16

    def compress(base, size, seeded, acc):
        def some(i, acc):
            for u in range(unroll):
                k = base + i * unroll + u
                c = meta[0, k]
                value = raws[seeded][lax.shift_right_logical(c, 1) & (half - 1)].astype(f32)
                begins = (c & 1) == 1
                if seeded:
                    begin = seeds[lax.shift_right_logical(c, 10)].astype(f32)
                    acc = jnp.where(begins, begin, acc) + value
                    slots[k] = acc.astype(bf16)
                else:
                    acc = jnp.where(begins, value, acc + value)
                    slots[k] = acc.astype(bf16)
                    seeds[k] = acc.astype(bf16)
            return acc

        return lax.fori_loop(0, size // unroll, some, acc)

    tile_loads[0].wait()
    acc = compress(0, half, False, jnp.zeros((BLK, BLK), f32))
    tile_loads[1].wait()
    quarter = half // 4
    for n in range(4):
        acc = compress(half + n * quarter, quarter, True, acc)
        for d in ((), (), (1, 3), (2,))[n]:
            near[d - 1].wait_recv()
            other = lax.rem(y + 4 - d, 4) * 2 + core
            side.append(send(xg.at[other], xg.at[other], side_sem + d, dcore=1))
    for copy in side:
        copy.wait_recv()

    sem_a, sem_b = take(12), take(12)

    def a_copy(q, xq, d):
        zt = lax.rem(z + d, 4)
        return remote(part.at[xq, 0, zt], recv_a.at[q, zt], sem_a + q * 4 + d, dx=q + 1)

    def b_copy(q, xq, d):
        return remote(
            part.at[xq, 1, lax.rem(z + d, 4)], recv_b.at[d - 1, xq], sem_b + q * 3 + d - 1, dz=d
        )

    def tile(r, c):
        return slots[meta[1, r * 16 + c]]

    def forward(q, carry):
        xq = lax.rem(x + 1 + q, 4)
        lhs = jnp.concatenate(
            [
                jnp.concatenate([tile(2 * (4 * xq + zz) + h, c) for c in range(16)], axis=1)
                for h in range(2)
                for zz in range(4)
            ],
            axis=0,
        )
        source = xg[...].reshape(16 * BLK, BLK)
        product = jnp.dot(lhs, source, preferred_element_type=f32)
        part[xq] = product.astype(bf16).reshape(2, 4, BLK, BLK)

        @pl.when(q < 3)
        def _():
            for d in (1, 2, 3, 0):
                a_copy(q, xq, d).start()

        for d in (1, 2, 3):
            b_copy(q, xq, d).start()
        return carry

    lax.fori_loop(0, 4, forward, 0)
    xqs = [lax.rem(x + 1 + q, 4) for q in range(4)]
    for q in range(4):
        if q < 3:
            for d in range(4):
                sent.append(a_copy(q, xqs[q], d))
        for d in (1, 2, 3):
            sent.append(b_copy(q, xqs[q], d))

    second_a, second_b = take(3), take(3)
    got_a, got_b = [], []

    def b_sum(q):
        total = part[xqs[q], 1, z].astype(f32)
        for d in (1, 2, 3):
            b_copy(q, xqs[q], d).wait_recv()
            total = total + recv_b[d - 1, xqs[q]].astype(f32)
        return total

    for q in range(3):
        sum_b[q] = b_sum(q).astype(bf16)
        got_b.append(send(sum_b.at[q], recv_b2.at[q], second_b + q, dx=q + 1))

    def a_sum(d):
        zt = lax.rem(z + d, 4)
        total = part[x, 0, zt].astype(f32)
        for q in range(3):
            a_copy(q, xqs[q], d).wait_recv()
            total = total + recv_a[q, zt].astype(f32)
        return total

    for d in (1, 2, 3):
        sum_a[d - 1] = a_sum(d).astype(bf16)
        got_a.append(send(sum_a.at[d - 1], recv_a2.at[d - 1], second_a + d - 1, dz=d))
    half_b = b_sum(3)
    half_a = a_sum(0)
    for q in range(3):
        got_b[q].wait_recv()
        half_b = half_b + recv_b2[q].astype(f32)
    for q in range(3):
        got_a[q].wait_recv()
        half_a = half_a + recv_a2[q].astype(f32)
    aggregated = jnp.concatenate([half_a, half_b], axis=0)
    agg = aggregated.astype(bf16)

    weight_load.wait()
    bias_load.wait()
    cot_load.wait()
    pre = jnp.dot(agg, weight[...], preferred_element_type=f32) + bias[...]
    sigma = jax.nn.sigmoid(pre)
    slope = (cot[...].astype(f32) * sigma * (1.0 + pre * (1.0 - sigma))).astype(bf16)
    vertex = lax.dot_general(
        weight[...], slope, (((1,), (1,)), ((), ())), preferred_element_type=f32
    ).astype(bf16)
    grads[col, 0] = vertex[:, :BLK]
    grads[col, 1] = vertex[:, BLK:]

    sem_ax, sem_bz, sem_az, sem_bx = take(3), take(3), take(3), take(3)
    sem_af, sem_bf = take(9), take(9)
    own_a, own_b = grads.at[col, 0], grads.at[col, 1]
    ax, bz, az, bx = {}, {}, {}, {}
    near_first = (1, 3, 2)
    for d in near_first:
        ax[d] = send(own_a, own_a, sem_ax + d - 1, dx=d)
        bz[d] = send(own_b, own_b, sem_bz + d - 1, dz=d)
    for d in near_first:
        az[d] = send(own_a, own_a, sem_az + d - 1, dz=d)
        bx[d] = send(own_b, own_b, sem_bx + d - 1, dx=d)

    wide = slope.astype(f32)
    bias_part = wide[0:8]
    for n in range(1, wide.shape[0] // 8):
        bias_part = bias_part + wide[n * 8 : n * 8 + 8]
    weight_part = jnp.dot(
        jnp.transpose(agg.astype(f32)).astype(bf16), slope, preferred_element_type=f32
    )
    w_sem1, w_sem2, w_sem3, w_sem4, w_sem5, w_sem6 = (take(n) for n in (1, 3, 3, 3, 3, 1))
    for n in range(2):
        w1[n, 0:64] = weight_part[n * 64 : n * 64 + 64]
        w1[n, 64:72] = bias_part
    w_got1 = send(w1.at[1 - core], w1.at[2], w_sem1, dcore=1)
    out_ref[...] = (pre * sigma).astype(bf16)

    def in_order(me, own, received):
        total = None
        for n in range(4):
            term = own
            for d in (1, 2, 3):
                term = jnp.where(lax.rem(me + 4 - d, 4) == n, received[d - 1], term)
            total = term if total is None else total + term
        return total

    w_got1.wait_recv()
    pair = w1[core] + w1[2]
    for n in range(4):
        w2[n, 0:16] = pair[n * 16 : n * 16 + 16]
        w2[n, 16:24] = pair[64:72]
    w_got2 = [
        send(w2.at[lax.rem(y + d, 4)], w2.at[3 + d], w_sem2 + d - 1, dy=d) for d in (1, 2, 3)
    ]

    af, bf = {}, {}
    for e in near_first:
        ax[e].wait_recv()
        bz[e].wait_recv()
    for d in near_first:
        for e in near_first:
            from_x = grads.at[lax.rem(x + 4 - e, 4) * 4 + z, 0]
            from_z = grads.at[x * 4 + lax.rem(z + 4 - e, 4), 1]
            af[e, d] = send(from_x, from_x, sem_af + (e - 1) * 3 + d - 1, dz=d)
            bf[e, d] = send(from_z, from_z, sem_bf + (e - 1) * 3 + d - 1, dx=d)

    for copy in w_got2:
        copy.wait_recv()
    w3[0] = in_order(y, w2[y], [w2[3 + d] for d in (1, 2, 3)])
    w_got3 = [send(w3.at[0], w3.at[d], w_sem3 + d - 1, dx=d) for d in (1, 2, 3)]

    def group(g):
        zg, xg_ = lax.rem(z + 4 - g, 4), lax.rem(x + 4 - g, 4)
        return [(xx * 4 + zg, 0) for xx in range(4)] + [(xg_ * 4 + zz, 1) for zz in range(4)]

    def backward(g, i):
        members = group(g)
        lhs = jnp.concatenate([grads[j, h] for j, h in members], axis=1)
        rhs = jnp.concatenate(
            [
                jnp.concatenate([tile(2 * j + h, 2 * i + b) for b in range(2)], axis=1)
                for j, h in members
            ],
            axis=0,
        )
        return jnp.dot(lhs, rhs, preferred_element_type=f32)

    WIDE = 4

    def run_group(g, fresh):
        def some(m, carry):
            for u in range(WIDE):
                i = m * WIDE + u
                back[i] = backward(g, i) if fresh else back[i] + backward(g, i)
            return carry

        lax.fori_loop(0, 8 // WIDE, some, 0)

    def arrive(g):
        az[g].wait_recv()
        bx[g].wait_recv()
        for e in (1, 2, 3):
            af[e, g].wait_recv()
            bf[e, g].wait_recv()

    run_group(0, True)
    arrive(1)
    run_group(1, False)
    arrive(3)

    for copy in w_got3:
        copy.wait_recv()
    w4[0] = in_order(x, w3[0], [w3[d] for d in (1, 2, 3)])
    w_got4 = [send(w4.at[0], w4.at[d], w_sem4 + d - 1, dz=d) for d in (1, 2, 3)]
    run_group(3, False)

    arrive(2)
    rs_sem1, rs_sem2 = take(4), take(3)
    order = (2, 1, 3, 0)
    got1 = []
    for n, d in enumerate(order):
        r = lax.rem(y + d, 4) * 2 + (1 - core)
        rs1_out[n] = (back[r] + backward(2, r)).astype(bf16)
        got1.append(send(rs1_out.at[n], rs1_in.at[n], rs_sem1 + n, dcore=1))
    got2 = []
    own = []
    for d in order:
        r = lax.rem(y + d, 4) * 2 + core
        own.append(back[r] + backward(2, r))
    for n, d in enumerate(order):
        got1[n].wait_recv()
        total = own[n] + rs1_in[n].astype(f32)
        if d:
            rs2_out[n] = total.astype(bf16)
            got2.append(send(rs2_out.at[n], rs2_in.at[n], rs_sem2 + n, dy=d))

    for copy in w_got4:
        copy.wait_recv()
    summed = in_order(z, w4[0], [w4[d] for d in (1, 2, 3)])
    scale = 1.0 / math.sqrt(256 * lax.axis_size("row") * lax.axis_size("col"))
    w5[core, y] = summed[0:16] * scale
    w_got5 = [send(w5.at[core, y], w5.at[core, y], w_sem5 + d - 1, dy=d) for d in (1, 2, 3)]
    bgrad_ref[...] = jnp.sum(summed[16:24], axis=0, keepdims=True) * scale
    for copy in w_got5:
        copy.wait_recv()
    w_got6 = send(w5.at[core], w5.at[core], w_sem6, dcore=1)

    for n in range(3):
        got2[n].wait_recv()
        total = total + rs2_in[n].astype(f32)
    fgrad_ref[...] = jnp.transpose(total)
    w_got6.wait_recv()
    wgrad_ref[...] = w5[...].reshape(128, 256)
    for copy in sent:
        copy.wait_send()
    assert counter[0] <= SEMS, counter[0]


SEMS = 112


def local(features, tile_values, tile_coords, tile_count, weight, bias, cotangent):
    tiles = tile_values.shape[2]
    vmem = pl.BlockSpec(memory_space=pltpu.VMEM)
    anywhere = pl.BlockSpec(memory_space=pl.ANY)
    square = (BLK, BLK)
    out, wgrad, bgrad, fgrad = pl.pallas_call(
        kernel,
        name="graph_layer",
        out_shape=(
            pltpu.VMEM((256, 256), bf16),
            pltpu.VMEM((128, 256), f32),
            pltpu.VMEM((1, 256), f32),
            pltpu.VMEM((256, 128), f32),
        ),
        in_specs=[pl.BlockSpec(memory_space=pltpu.HBM)] * 7,
        out_specs=(vmem, vmem, vmem, vmem),
        scratch_shapes=[
            pltpu.VMEM((tiles // 2, *square), bf16),
            pltpu.VMEM((tiles // 2, *square), bf16),
            pltpu.VMEM((tiles + 1, *square), bf16),
            pltpu.VMEM((tiles // 2 + 1, *square), bf16),
            pltpu.VMEM((8, 256, 128), bf16),
            pltpu.VMEM((2, tiles), i32),
            pltpu.VMEM((1, 1), i32),
            pltpu.VMEM((128, 256), bf16),
            pltpu.VMEM((1, 256), f32),
            pltpu.VMEM((256, 256), bf16),
            pltpu.VMEM((2, tiles), i32),
            pltpu.SMEM((2, tiles), i32),
            pltpu.VMEM((4, 2, 4, *square), bf16),
            pltpu.VMEM((3, 4, *square), bf16),
            pltpu.VMEM((3, 4, *square), bf16),
            pltpu.VMEM((3, *square), bf16),
            pltpu.VMEM((3, *square), bf16),
            pltpu.VMEM((3, *square), bf16),
            pltpu.VMEM((3, *square), bf16),
            pltpu.VMEM((16, 2, *square), bf16),
            pltpu.VMEM((8, 128, 256), f32),
            pltpu.VMEM((4, 128, 256), bf16),
            pltpu.VMEM((4, 128, 256), bf16),
            pltpu.VMEM((3, 128, 256), bf16),
            pltpu.VMEM((3, 128, 256), bf16),
            pltpu.VMEM((3, 72, 256), f32),
            pltpu.VMEM((7, 24, 256), f32),
            pltpu.VMEM((4, 24, 256), f32),
            pltpu.VMEM((4, 24, 256), f32),
            pltpu.VMEM((2, 4, 16, 256), f32),
            pltpu.SemaphoreType.DMA((8,)),
            pltpu.SemaphoreType.DMA((SEMS,)),
            pltpu.SemaphoreType.DMA((SEMS,)),
        ],
        compiler_params=pltpu.CompilerParams(
            collective_id=0, has_side_effects=True, vmem_limit_bytes=56 * 2**20
        ),
    )(features, tile_values, tile_coords, tile_count, weight, bias.reshape(1, 256), cotangent)
    kinds = (((256, 256), bf16), ((128, 256), f32), ((1, 256), f32), ((256, 128), f32))
    out, wgrad, bgrad, fgrad = pl.pallas_call(
        finish,
        name="finish",
        out_shape=[jax.ShapeDtypeStruct(*kind) for kind in kinds],
        in_specs=[anywhere] * 4,
        out_specs=[anywhere] * 4,
        scratch_shapes=[pltpu.SemaphoreType.DMA((4,))],
    )(*(pltpu.with_memory_space_constraint(v, pltpu.VMEM) for v in (out, wgrad, bgrad, fgrad)))
    return out, wgrad, bgrad.reshape(256), fgrad


def finish(*refs):
    sems = refs[-1]
    copies = [pltpu.make_async_copy(refs[n], refs[4 + n], sems.at[n]) for n in range(4)]
    for copy in copies:
        copy.start()
    for copy in copies:
        copy.wait()


def solution(mesh):
    placed = (
        P(("row", "col"), None),
        P("row", "col", None, None, None),
        P("row", "col", None, None),
        P("row", "col"),
        P(),
        P(),
        P(("row", "col"), None),
    )
    return jax.shard_map(
        local,
        mesh=mesh,
        in_specs=placed,
        out_specs=(P(("row", "col"), None), P(), P(), P(("row", "col"), None)),
        check_vma=False,
    )
```

```python
import functools
import math

import jax
import jax.numpy as jnp
from jax import lax
from jax.experimental import pallas as pl
from jax.experimental.pallas import tpu as pltpu
from jax.sharding import PartitionSpec as P

f32, bf16, i32 = jnp.float32, jnp.bfloat16, jnp.int32
MESH = pl.DeviceIdType.MESH
BLK = 128


def kernel(
    feats_hbm, tiles_hbm, coords_hbm, count_hbm, weight_hbm, bias_hbm, cot_hbm,
    out_ref, wgrad_ref, bgrad_ref, fgrad_ref,
    raw0, raw1, slots, seeds, xg, coords, alive, weight, bias, cot, meta_v, meta,
    part, recv_a, recv_b, sum_a, sum_b, recv_a2, recv_b2,
    grads, back, rs1_out, rs1_in, rs2_out, rs2_in,
    w1, w2, w3, w4, w5,
    load_sem, send_sem, recv_sem,
):
    raws = (raw0, raw1)
    tiles = 2 * raw0.shape[0]
    row, col = lax.axis_index("row"), lax.axis_index("col")
    y, core = lax.div(row, 2), lax.rem(row, 2)
    x, z = lax.div(col, 4), lax.rem(col, 4)

    def device(dy=0, dcore=0, dx=0, dz=0):
        return (
            lax.rem(y + dy, 4) * 2 + lax.rem(core + dcore, 2),
            lax.rem(x + dx, 4) * 4 + lax.rem(z + dz, 4),
        )

    counter = [0]

    def remote(src, dst, sem, **where):
        return pltpu.make_async_remote_copy(
            src_ref=src,
            dst_ref=dst,
            send_sem=send_sem.at[sem],
            recv_sem=recv_sem.at[sem],
            device_id=device(**where),
            device_id_type=MESH,
        )

    def take(count):
        first = counter[0]
        counter[0] += count
        return first

    sent = []

    def send(*args, **where):
        copy = remote(*args, **where)
        copy.start()
        sent.append(copy)
        return copy

    def load(src, dst, sem):
        copy = pltpu.make_async_copy(src, dst, load_sem.at[sem])
        copy.start()
        return copy

    half = tiles // 2
    coords_load = load(coords_hbm.at[0, 0], coords, 0)
    count_load = load(count_hbm, alive, 1)
    feats_load = load(feats_hbm, xg.at[row], 2)
    tile_loads = [
        load(tiles_hbm.at[0, 0, pl.ds(n * half, half)], raws[n], 3 + n)
        for n in range(2)
    ]
    weight_load = load(weight_hbm, weight, 5)
    bias_load = load(bias_hbm, bias, 6)
    cot_load = load(cot_hbm, cot, 7)

    barrier = pltpu.get_barrier_semaphore()
    peers = [device(dcore=1)]
    for d in (1, 2, 3):
        peers += [device(dy=d), device(dx=d), device(dz=d)]
    for peer in peers:
        pl.semaphore_signal(barrier, inc=1, device_id=peer, device_id_type=MESH)

    slots[tiles] = jnp.zeros((BLK, BLK), bf16)
    seeds[half] = jnp.zeros((BLK, BLK), bf16)
    coords_load.wait()
    count_load.wait()
    lanes = lax.broadcasted_iota(i32, (1, tiles), 1)
    pos = jnp.where(lanes < alive[...], coords[0:1, :] * 16 + coords[1:2, :], tiles)

    def down(v):
        return jnp.transpose(jnp.broadcast_to(v, (BLK, v.shape[1])))

    def count(mask):
        return jnp.sum(jnp.where(mask, 1, 0), axis=0, keepdims=True)

    key = pos * tiles + lanes
    ranks, firsts = [], []
    pos_down, key_down = down(pos), down(key)
    for n in range(tiles // BLK):
        cut = slice(n * BLK, (n + 1) * BLK)
        same = slice(0, half) if n < tiles // BLK // 2 else slice(half, tiles)
        before = key_down[same] < key[:, cut]
        ranks.append(count(before))
        firsts.append(count(before & (pos_down[same] == pos[:, cut])))

    rank = jnp.concatenate(ranks, axis=1)
    first = jnp.where(jnp.concatenate(firsts, axis=1) == 0, 1, 0)
    seed = []
    for n in range(tiles // BLK):
        cut = slice(n * BLK, (n + 1) * BLK)
        if n < tiles // BLK // 2:
            seed.append(jnp.full((1, BLK), half, i32))
        else:
            upto, here = count(pos_down[:half] <= pos[:, cut]), count(pos_down[:half] == pos[:, cut])
            seed.append(jnp.where(here == 0, half, upto - 1))
    code = (jnp.concatenate(seed, axis=1) * tiles + lanes) * 2 + first
    rank_down, code_down = down(rank), down(code)
    for n in range(tiles // BLK):
        cut = slice(n * BLK, (n + 1) * BLK)
        at = lanes[:, cut]
        same = slice(0, half) if n < tiles // BLK // 2 else slice(half, tiles)
        slot = at if n < tiles // BLK // 2 else at - half
        meta_v[0:1, cut] = jnp.sum(
            jnp.where(rank_down[same] == slot, code_down[same], 0), axis=0, keepdims=True
        )
        upto0, here0 = count(pos_down[:half] <= at), count(pos_down[:half] == at)
        upto1, here1 = count(pos_down[half:] <= at), count(pos_down[half:] == at)
        early = jnp.where(here0 == 0, tiles, upto0 - 1)
        meta_v[1:2, cut] = jnp.where(here1 == 0, early, half + upto1 - 1)
    meta_load = load(meta_v, meta, 0)
    meta_load.wait()

    unroll = 16

    def compress(base, size, seeded, acc):
        def some(i, acc):
            for u in range(unroll):
                k = base + i * unroll + u
                c = meta[0, k]
                value = raws[seeded][lax.shift_right_logical(c, 1) & (half - 1)].astype(f32)
                begins = (c & 1) == 1
                if seeded:
                    begin = seeds[lax.shift_right_logical(c, 10)].astype(f32)
                    acc = jnp.where(begins, begin, acc) + value
                    slots[k] = acc.astype(bf16)
                else:
                    acc = jnp.where(begins, value, acc + value)
                    slots[k] = acc.astype(bf16)
                    seeds[k] = acc.astype(bf16)
            return acc

        return lax.fori_loop(0, size // unroll, some, acc)

    tile_loads[0].wait()
    early = half // 2
    acc = compress(0, early, False, jnp.zeros((BLK, BLK), f32))

    pl.semaphore_wait(barrier, len(peers))
    feats_load.wait()
    sem = take(3)
    near = [send(xg.at[row], xg.at[row], sem + d - 1, dy=d) for d in (1, 2, 3)]
    side_sem = take(4)
    side = [send(xg.at[row], xg.at[row], side_sem, dcore=1)]

    acc = compress(early, half - early, False, acc)
    tile_loads[1].wait()
    compress(half, half, True, acc)
    for d in (1, 3, 2):
        near[d - 1].wait_recv()
        other = lax.rem(y + 4 - d, 4) * 2 + core
        side.append(send(xg.at[other], xg.at[other], side_sem + d, dcore=1))
    for copy in side:
        copy.wait_recv()

    sem_a, sem_b = take(12), take(12)

    def turn(q):
        if isinstance(q, int):
            return (2, 1, 3, 0)[q]
        return 2 - q + 3 * lax.div(q, 2) - 2 * lax.div(q, 3)

    def a_copy(q, xq, d):
        zt = lax.rem(z + d, 4)
        return remote(part.at[xq, 0, zt], recv_a.at[q, zt], sem_a + q * 4 + d, dx=turn(q))

    def b_copy(q, xq, d):
        return remote(
            part.at[xq, 1, lax.rem(z + d, 4)], recv_b.at[d - 1, xq], sem_b + q * 3 + d - 1, dz=d
        )

    def tile(r, c):
        return slots[meta[1, r * 16 + c]]

    def forward(q, carry):
        xq = lax.rem(x + turn(q), 4)
        lhs = jnp.concatenate(
            [
                jnp.concatenate([tile(2 * (4 * xq + zz) + h, c) for c in range(16)], axis=1)
                for h in range(2)
                for zz in range(4)
            ],
            axis=0,
        )
        source = xg[...].reshape(16 * BLK, BLK)
        product = jnp.dot(lhs, source, preferred_element_type=f32)
        part[xq] = product.astype(bf16).reshape(2, 4, BLK, BLK)

        @pl.when(q < 3)
        def _():
            for d in (1, 2, 3, 0):
                a_copy(q, xq, d).start()

        for d in (1, 2, 3):
            b_copy(q, xq, d).start()
        return carry

    lax.fori_loop(0, 4, forward, 0)
    xqs = [lax.rem(x + turn(q), 4) for q in range(4)]
    for q in range(4):
        if q < 3:
            for d in range(4):
                sent.append(a_copy(q, xqs[q], d))
        for d in (1, 2, 3):
            sent.append(b_copy(q, xqs[q], d))

    second_a, second_b = take(3), take(3)
    got_a, got_b = [], []

    def b_sum(q):
        total = part[xqs[q], 1, z].astype(f32)
        for d in (1, 2, 3):
            b_copy(q, xqs[q], d).wait_recv()
            total = total + recv_b[d - 1, xqs[q]].astype(f32)
        return total

    for q in range(3):
        sum_b[q] = b_sum(q).astype(bf16)
        got_b.append(send(sum_b.at[q], recv_b2.at[q], second_b + q, dx=turn(q)))

    def a_sum(d):
        zt = lax.rem(z + d, 4)
        total = part[x, 0, zt].astype(f32)
        for q in range(3):
            a_copy(q, xqs[q], d).wait_recv()
            total = total + recv_a[q, zt].astype(f32)
        return total

    for d in (1, 2, 3):
        sum_a[d - 1] = a_sum(d).astype(bf16)
        got_a.append(send(sum_a.at[d - 1], recv_a2.at[d - 1], second_a + d - 1, dz=d))
    half_b = b_sum(3)
    half_a = a_sum(0)
    for q in range(3):
        got_b[q].wait_recv()
        half_b = half_b + recv_b2[q].astype(f32)
    for q in range(3):
        got_a[q].wait_recv()
        half_a = half_a + recv_a2[q].astype(f32)
    aggregated = jnp.concatenate([half_a, half_b], axis=0)
    agg = aggregated.astype(bf16)

    weight_load.wait()
    bias_load.wait()
    cot_load.wait()
    pre = jnp.dot(agg, weight[...], preferred_element_type=f32) + bias[...]
    sigma = jax.nn.sigmoid(pre)
    slope = (cot[...].astype(f32) * sigma * (1.0 + pre * (1.0 - sigma))).astype(bf16)
    vertex = lax.dot_general(
        weight[...], slope, (((1,), (1,)), ((), ())), preferred_element_type=f32
    ).astype(bf16)
    grads[col, 0] = vertex[:, :BLK]
    grads[col, 1] = vertex[:, BLK:]

    sem_ax, sem_bz, sem_az, sem_bx = take(3), take(3), take(3), take(3)
    sem_af, sem_bf = take(9), take(9)
    own_a, own_b = grads.at[col, 0], grads.at[col, 1]
    ax, bz, az, bx = {}, {}, {}, {}
    near_first = (1, 3, 2)
    for d in near_first:
        ax[d] = send(own_a, own_a, sem_ax + d - 1, dx=d)
        bz[d] = send(own_b, own_b, sem_bz + d - 1, dz=d)
    for d in near_first:
        az[d] = send(own_a, own_a, sem_az + d - 1, dz=d)
        bx[d] = send(own_b, own_b, sem_bx + d - 1, dx=d)

    wide = slope.astype(f32)
    bias_part = wide[0:8]
    for n in range(1, wide.shape[0] // 8):
        bias_part = bias_part + wide[n * 8 : n * 8 + 8]
    weight_part = jnp.dot(
        jnp.transpose(agg.astype(f32)).astype(bf16), slope, preferred_element_type=f32
    )
    w_sem1, w_sem2, w_sem3, w_sem4, w_sem5, w_sem6 = (take(n) for n in (1, 3, 3, 3, 3, 1))
    for n in range(2):
        w1[n, 0:64] = weight_part[n * 64 : n * 64 + 64]
        w1[n, 64:72] = bias_part
    w_got1 = send(w1.at[1 - core], w1.at[2], w_sem1, dcore=1)
    out_ref[...] = (pre * sigma).astype(bf16)

    def in_order(me, own, received):
        total = None
        for n in range(4):
            term = own
            for d in (1, 2, 3):
                term = jnp.where(lax.rem(me + 4 - d, 4) == n, received[d - 1], term)
            total = term if total is None else total + term
        return total

    w_got1.wait_recv()
    pair = w1[core] + w1[2]
    for n in range(4):
        w2[n, 0:16] = pair[n * 16 : n * 16 + 16]
        w2[n, 16:24] = pair[64:72]
    w_got2 = [
        send(w2.at[lax.rem(y + d, 4)], w2.at[3 + d], w_sem2 + d - 1, dy=d) for d in (1, 2, 3)
    ]

    af, bf = {}, {}
    for e in near_first:
        ax[e].wait_recv()
        bz[e].wait_recv()

    def forward_to(d):
        for e in near_first:
            from_x = grads.at[lax.rem(x + 4 - e, 4) * 4 + z, 0]
            from_z = grads.at[x * 4 + lax.rem(z + 4 - e, 4), 1]
            af[e, d] = send(from_x, from_x, sem_af + (e - 1) * 3 + d - 1, dz=d)
            bf[e, d] = send(from_z, from_z, sem_bf + (e - 1) * 3 + d - 1, dx=d)

    forward_to(1)
    forward_to(3)

    for copy in w_got2:
        copy.wait_recv()
    w3[0] = in_order(y, w2[y], [w2[3 + d] for d in (1, 2, 3)])
    w_got3 = [send(w3.at[0], w3.at[d], w_sem3 + d - 1, dx=d) for d in (1, 2, 3)]
    forward_to(2)

    def group(g):
        zg, xg_ = lax.rem(z + 4 - g, 4), lax.rem(x + 4 - g, 4)
        return [(xx * 4 + zg, 0) for xx in range(4)] + [(xg_ * 4 + zz, 1) for zz in range(4)]

    def backward(g, i):
        members = group(g)
        lhs = jnp.concatenate([grads[j, h] for j, h in members], axis=1)
        rhs = jnp.concatenate(
            [
                jnp.concatenate([tile(2 * j + h, 2 * i + b) for b in range(2)], axis=1)
                for j, h in members
            ],
            axis=0,
        )
        return jnp.dot(lhs, rhs, preferred_element_type=f32)

    WIDE = 4

    def run_group(g, fresh):
        def some(m, carry):
            for u in range(WIDE):
                i = m * WIDE + u
                back[i] = backward(g, i) if fresh else back[i] + backward(g, i)
            return carry

        lax.fori_loop(0, 8 // WIDE, some, 0)

    def arrive(g):
        az[g].wait_recv()
        bx[g].wait_recv()
        for e in (1, 2, 3):
            af[e, g].wait_recv()
            bf[e, g].wait_recv()

    run_group(0, True)
    arrive(1)

    run_group(1, False)

    for copy in w_got3:
        copy.wait_recv()
    w4[0] = in_order(x, w3[0], [w3[d] for d in (1, 2, 3)])
    w_got4 = [send(w4.at[0], w4.at[d], w_sem4 + d - 1, dz=d) for d in (1, 2, 3)]

    arrive(3)
    run_group(3, False)

    arrive(2)
    rs_sem1, rs_sem2 = take(4), take(3)
    order = (2, 1, 3, 0)
    got1 = []
    for n, d in enumerate(order):
        r = lax.rem(y + d, 4) * 2 + (1 - core)
        rs1_out[n] = (back[r] + backward(2, r)).astype(bf16)
        got1.append(send(rs1_out.at[n], rs1_in.at[n], rs_sem1 + n, dcore=1))
    for copy in w_got4:
        copy.wait_recv()
    summed = in_order(z, w4[0], [w4[d] for d in (1, 2, 3)])
    scale = 1.0 / math.sqrt(256 * lax.axis_size("row") * lax.axis_size("col"))
    w5[core, y] = summed[0:16] * scale
    w_got5 = [send(w5.at[core, y], w5.at[core, y], w_sem5 + d - 1, dy=d) for d in (1, 2, 3)]
    bgrad_ref[...] = jnp.sum(summed[16:24], axis=0, keepdims=True) * scale

    got2 = []
    own = []
    for d in order:
        r = lax.rem(y + d, 4) * 2 + core
        own.append(back[r] + backward(2, r))
    for n, d in enumerate(order):
        got1[n].wait_recv()
        total = own[n] + rs1_in[n].astype(f32)
        if d:
            rs2_out[n] = total.astype(bf16)
            got2.append(send(rs2_out.at[n], rs2_in.at[n], rs_sem2 + n, dy=d))

    for copy in w_got5:
        copy.wait_recv()
    w_got6 = send(w5.at[core], w5.at[core], w_sem6, dcore=1)

    for n in range(3):
        got2[n].wait_recv()
        total = total + rs2_in[n].astype(f32)
    fgrad_ref[...] = jnp.transpose(total)
    w_got6.wait_recv()
    wgrad_ref[...] = w5[...].reshape(128, 256)
    for copy in sent:
        copy.wait_send()
    assert counter[0] <= SEMS, counter[0]


SEMS = 112


def local(features, tile_values, tile_coords, tile_count, weight, bias, cotangent):
    tiles = tile_values.shape[2]
    vmem = pl.BlockSpec(memory_space=pltpu.VMEM)
    anywhere = pl.BlockSpec(memory_space=pl.ANY)
    square = (BLK, BLK)
    out, wgrad, bgrad, fgrad = pl.pallas_call(
        kernel,
        name="graph_layer",
        out_shape=(
            pltpu.VMEM((256, 256), bf16),
            pltpu.VMEM((128, 256), f32),
            pltpu.VMEM((1, 256), f32),
            pltpu.VMEM((256, 128), f32),
        ),
        in_specs=[pl.BlockSpec(memory_space=pltpu.HBM)] * 7,
        out_specs=(vmem, vmem, vmem, vmem),
        scratch_shapes=[
            pltpu.VMEM((tiles // 2, *square), bf16),
            pltpu.VMEM((tiles // 2, *square), bf16),
            pltpu.VMEM((tiles + 1, *square), bf16),
            pltpu.VMEM((tiles // 2 + 1, *square), bf16),
            pltpu.VMEM((8, 256, 128), bf16),
            pltpu.VMEM((2, tiles), i32),
            pltpu.VMEM((1, 1), i32),
            pltpu.VMEM((128, 256), bf16),
            pltpu.VMEM((1, 256), f32),
            pltpu.VMEM((256, 256), bf16),
            pltpu.VMEM((2, tiles), i32),
            pltpu.SMEM((2, tiles), i32),
            pltpu.VMEM((4, 2, 4, *square), bf16),
            pltpu.VMEM((3, 4, *square), bf16),
            pltpu.VMEM((3, 4, *square), bf16),
            pltpu.VMEM((3, *square), bf16),
            pltpu.VMEM((3, *square), bf16),
            pltpu.VMEM((3, *square), bf16),
            pltpu.VMEM((3, *square), bf16),
            pltpu.VMEM((16, 2, *square), bf16),
            pltpu.VMEM((8, 128, 256), f32),
            pltpu.VMEM((4, 128, 256), bf16),
            pltpu.VMEM((4, 128, 256), bf16),
            pltpu.VMEM((3, 128, 256), bf16),
            pltpu.VMEM((3, 128, 256), bf16),
            pltpu.VMEM((3, 72, 256), f32),
            pltpu.VMEM((7, 24, 256), f32),
            pltpu.VMEM((4, 24, 256), f32),
            pltpu.VMEM((4, 24, 256), f32),
            pltpu.VMEM((2, 4, 16, 256), f32),
            pltpu.SemaphoreType.DMA((8,)),
            pltpu.SemaphoreType.DMA((SEMS,)),
            pltpu.SemaphoreType.DMA((SEMS,)),
        ],
        compiler_params=pltpu.CompilerParams(
            collective_id=0, has_side_effects=True, vmem_limit_bytes=56 * 2**20
        ),
    )(features, tile_values, tile_coords, tile_count, weight, bias.reshape(1, 256), cotangent)
    kinds = (((256, 256), bf16), ((128, 256), f32), ((1, 256), f32), ((256, 128), f32))
    out, wgrad, bgrad, fgrad = pl.pallas_call(
        finish,
        name="finish",
        out_shape=[jax.ShapeDtypeStruct(*kind) for kind in kinds],
        in_specs=[anywhere] * 4,
        out_specs=[anywhere] * 4,
        scratch_shapes=[pltpu.SemaphoreType.DMA((4,))],
    )(*(pltpu.with_memory_space_constraint(v, pltpu.VMEM) for v in (out, wgrad, bgrad, fgrad)))
    return out, wgrad, bgrad.reshape(256), fgrad


def finish(*refs):
    sems = refs[-1]
    copies = [pltpu.make_async_copy(refs[n], refs[4 + n], sems.at[n]) for n in range(4)]
    for copy in copies:
        copy.start()
    for copy in copies:
        copy.wait()


def solution(mesh):
    placed = (
        P(("row", "col"), None),
        P("row", "col", None, None, None),
        P("row", "col", None, None),
        P("row", "col"),
        P(),
        P(),
        P(("row", "col"), None),
    )
    return jax.shard_map(
        local,
        mesh=mesh,
        in_specs=placed,
        out_specs=(P(("row", "col"), None), P(), P(), P(("row", "col"), None)),
        check_vma=False,
    )
```

```python
import functools
import math

import jax
import jax.numpy as jnp
from jax import lax
from jax.experimental import pallas as pl
from jax.experimental.pallas import tpu as pltpu
from jax.sharding import PartitionSpec as P

f32, bf16, i32 = jnp.float32, jnp.bfloat16, jnp.int32
MESH = pl.DeviceIdType.MESH
BLK = 128


def kernel(
    feats_hbm, tiles_hbm, coords_hbm, count_hbm, weight_hbm, bias_hbm, cot_hbm,
    out_ref, wgrad_ref, bgrad_ref, fgrad_ref,
    raw0, raw1, slots, seeds, xg, coords, alive, weight, bias, cot, meta_v, meta,
    part, recv_a, recv_b, sum_a, sum_b, recv_a2, recv_b2,
    grads, back, rs1_out, rs1_in, rs2_out, rs2_in,
    w1, w2, w3, w4, w5,
    load_sem, send_sem, recv_sem,
):
    raws = (raw0, raw1)
    tiles = 2 * raw0.shape[0]
    row, col = lax.axis_index("row"), lax.axis_index("col")
    y, core = lax.div(row, 2), lax.rem(row, 2)
    x, z = lax.div(col, 4), lax.rem(col, 4)

    def device(dy=0, dcore=0, dx=0, dz=0):
        return (
            lax.rem(y + dy, 4) * 2 + lax.rem(core + dcore, 2),
            lax.rem(x + dx, 4) * 4 + lax.rem(z + dz, 4),
        )

    counter = [0]

    def remote(src, dst, sem, **where):
        return pltpu.make_async_remote_copy(
            src_ref=src,
            dst_ref=dst,
            send_sem=send_sem.at[sem],
            recv_sem=recv_sem.at[sem],
            device_id=device(**where),
            device_id_type=MESH,
        )

    def take(count):
        first = counter[0]
        counter[0] += count
        return first

    sent = []

    def send(*args, **where):
        copy = remote(*args, **where)
        copy.start()
        sent.append(copy)
        return copy

    def load(src, dst, sem):
        copy = pltpu.make_async_copy(src, dst, load_sem.at[sem])
        copy.start()
        return copy

    half = tiles // 2
    coords_load = load(coords_hbm.at[0, 0], coords, 0)
    count_load = load(count_hbm, alive, 1)
    feats_load = load(feats_hbm, xg.at[row], 2)
    tile_loads = [
        load(tiles_hbm.at[0, 0, pl.ds(n * half, half)], raws[n], 3 + n)
        for n in range(2)
    ]
    weight_load = load(weight_hbm, weight, 5)
    bias_load = load(bias_hbm, bias, 6)
    cot_load = load(cot_hbm, cot, 7)

    barrier = pltpu.get_barrier_semaphore()
    peers = [device(dcore=1)]
    for d in (1, 2, 3):
        peers += [device(dy=d), device(dy=d, dcore=1), device(dx=d), device(dz=d)]
    for peer in peers:
        pl.semaphore_signal(barrier, inc=1, device_id=peer, device_id_type=MESH)

    slots[tiles] = jnp.zeros((BLK, BLK), bf16)
    seeds[half] = jnp.zeros((BLK, BLK), bf16)
    coords_load.wait()
    count_load.wait()
    lanes = lax.broadcasted_iota(i32, (1, tiles), 1)
    pos = jnp.where(lanes < alive[...], coords[0:1, :] * 16 + coords[1:2, :], tiles)

    def down(v):
        return jnp.transpose(jnp.broadcast_to(v, (BLK, v.shape[1])))

    def count(mask):
        return jnp.sum(jnp.where(mask, 1, 0), axis=0, keepdims=True)

    key = pos * tiles + lanes
    ranks, firsts = [], []
    pos_down, key_down = down(pos), down(key)
    for n in range(tiles // BLK):
        cut = slice(n * BLK, (n + 1) * BLK)
        same = slice(0, half) if n < tiles // BLK // 2 else slice(half, tiles)
        before = key_down[same] < key[:, cut]
        ranks.append(count(before))
        firsts.append(count(before & (pos_down[same] == pos[:, cut])))

    rank = jnp.concatenate(ranks, axis=1)
    first = jnp.where(jnp.concatenate(firsts, axis=1) == 0, 1, 0)
    seed = []
    for n in range(tiles // BLK):
        cut = slice(n * BLK, (n + 1) * BLK)
        if n < tiles // BLK // 2:
            seed.append(jnp.full((1, BLK), half, i32))
        else:
            upto, here = count(pos_down[:half] <= pos[:, cut]), count(pos_down[:half] == pos[:, cut])
            seed.append(jnp.where(here == 0, half, upto - 1))
    code = (jnp.concatenate(seed, axis=1) * tiles + lanes) * 2 + first
    rank_down, code_down = down(rank), down(code)
    for n in range(tiles // BLK):
        cut = slice(n * BLK, (n + 1) * BLK)
        at = lanes[:, cut]
        same = slice(0, half) if n < tiles // BLK // 2 else slice(half, tiles)
        slot = at if n < tiles // BLK // 2 else at - half
        meta_v[0:1, cut] = jnp.sum(
            jnp.where(rank_down[same] == slot, code_down[same], 0), axis=0, keepdims=True
        )
        upto0, here0 = count(pos_down[:half] <= at), count(pos_down[:half] == at)
        upto1, here1 = count(pos_down[half:] <= at), count(pos_down[half:] == at)
        early = jnp.where(here0 == 0, tiles, upto0 - 1)
        meta_v[1:2, cut] = jnp.where(here1 == 0, early, half + upto1 - 1)
    meta_load = load(meta_v, meta, 0)
    meta_load.wait()

    unroll = 16

    def compress(base, size, seeded, acc):
        def some(i, acc):
            for u in range(unroll):
                k = base + i * unroll + u
                c = meta[0, k]
                value = raws[seeded][lax.shift_right_logical(c, 1) & (half - 1)].astype(f32)
                begins = (c & 1) == 1
                if seeded:
                    begin = seeds[lax.shift_right_logical(c, 10)].astype(f32)
                    acc = jnp.where(begins, begin, acc) + value
                    slots[k] = acc.astype(bf16)
                else:
                    acc = jnp.where(begins, value, acc + value)
                    slots[k] = acc.astype(bf16)
                    seeds[k] = acc.astype(bf16)
            return acc

        return lax.fori_loop(0, size // unroll, some, acc)

    tile_loads[0].wait()
    early = half // 2
    acc = compress(0, early, False, jnp.zeros((BLK, BLK), f32))

    pl.semaphore_wait(barrier, len(peers))
    feats_load.wait()
    sem = take(3)
    near = [send(xg.at[row], xg.at[row], sem + d - 1, dy=d) for d in (1, 2, 3)]
    side_sem = take(4)
    side = [send(xg.at[row], xg.at[row], side_sem, dcore=1)]

    acc = compress(early, half - early, False, acc)
    tile_loads[1].wait()
    compress(half, half, True, acc)
    for d in (1, 3, 2):
        near[d - 1].wait_recv()
        other = lax.rem(y + 4 - d, 4) * 2 + core
        side.append(send(xg.at[other], xg.at[other], side_sem + d, dcore=1))
    for copy in side:
        copy.wait_recv()

    sem_a, sem_b = take(12), take(12)

    def turn(q):
        if isinstance(q, int):
            return (2, 1, 3, 0)[q]
        return 2 - q + 3 * lax.div(q, 2) - 2 * lax.div(q, 3)

    def a_copy(q, xq, d):
        zt = lax.rem(z + d, 4)
        return remote(part.at[xq, 0, zt], recv_a.at[q, zt], sem_a + q * 4 + d, dx=turn(q))

    def b_copy(q, xq, d):
        return remote(
            part.at[xq, 1, lax.rem(z + d, 4)], recv_b.at[d - 1, xq], sem_b + q * 3 + d - 1, dz=d
        )

    def tile(r, c):
        return slots[meta[1, r * 16 + c]]

    def forward(q, carry):
        xq = lax.rem(x + turn(q), 4)
        lhs = jnp.concatenate(
            [
                jnp.concatenate([tile(2 * (4 * xq + zz) + h, c) for c in range(16)], axis=1)
                for h in range(2)
                for zz in range(4)
            ],
            axis=0,
        )
        source = xg[...].reshape(16 * BLK, BLK)
        product = jnp.dot(lhs, source, preferred_element_type=f32)
        part[xq] = product.astype(bf16).reshape(2, 4, BLK, BLK)

        @pl.when(q < 3)
        def _():
            for d in (1, 2, 3, 0):
                a_copy(q, xq, d).start()

        for d in (1, 2, 3):
            b_copy(q, xq, d).start()
        return carry

    lax.fori_loop(0, 4, forward, 0)
    xqs = [lax.rem(x + turn(q), 4) for q in range(4)]
    for q in range(4):
        if q < 3:
            for d in range(4):
                sent.append(a_copy(q, xqs[q], d))
        for d in (1, 2, 3):
            sent.append(b_copy(q, xqs[q], d))

    second_a, second_b = take(3), take(3)
    got_a, got_b = [], []

    def b_sum(q):
        total = part[xqs[q], 1, z].astype(f32)
        for d in (1, 2, 3):
            b_copy(q, xqs[q], d).wait_recv()
            total = total + recv_b[d - 1, xqs[q]].astype(f32)
        return total

    for q in range(3):
        sum_b[q] = b_sum(q).astype(bf16)
        got_b.append(send(sum_b.at[q], recv_b2.at[q], second_b + q, dx=turn(q)))

    def a_sum(d):
        zt = lax.rem(z + d, 4)
        total = part[x, 0, zt].astype(f32)
        for q in range(3):
            a_copy(q, xqs[q], d).wait_recv()
            total = total + recv_a[q, zt].astype(f32)
        return total

    for d in (1, 2, 3):
        sum_a[d - 1] = a_sum(d).astype(bf16)
        got_a.append(send(sum_a.at[d - 1], recv_a2.at[d - 1], second_a + d - 1, dz=d))
    half_b = b_sum(3)
    half_a = a_sum(0)
    for q in range(3):
        got_b[q].wait_recv()
        half_b = half_b + recv_b2[q].astype(f32)
    for q in range(3):
        got_a[q].wait_recv()
        half_a = half_a + recv_a2[q].astype(f32)
    aggregated = jnp.concatenate([half_a, half_b], axis=0)
    agg = aggregated.astype(bf16)

    weight_load.wait()
    bias_load.wait()
    cot_load.wait()
    pre = jnp.dot(agg, weight[...], preferred_element_type=f32) + bias[...]
    sigma = jax.nn.sigmoid(pre)
    slope = (cot[...].astype(f32) * sigma * (1.0 + pre * (1.0 - sigma))).astype(bf16)
    vertex = lax.dot_general(
        weight[...], slope, (((1,), (1,)), ((), ())), preferred_element_type=f32
    ).astype(bf16)
    grads[col, 0] = vertex[:, :BLK]
    grads[col, 1] = vertex[:, BLK:]

    sem_ax, sem_bz, sem_az, sem_bx = take(3), take(3), take(3), take(3)
    sem_af, sem_bf = take(9), take(9)
    own_a, own_b = grads.at[col, 0], grads.at[col, 1]
    ax, bz, az, bx = {}, {}, {}, {}
    near_first = (1, 3, 2)
    for d in near_first:
        ax[d] = send(own_a, own_a, sem_ax + d - 1, dx=d)
        bz[d] = send(own_b, own_b, sem_bz + d - 1, dz=d)
    for d in near_first:
        az[d] = send(own_a, own_a, sem_az + d - 1, dz=d)
        bx[d] = send(own_b, own_b, sem_bx + d - 1, dx=d)

    wide = slope.astype(f32)
    bias_part = wide[0:8]
    for n in range(1, wide.shape[0] // 8):
        bias_part = bias_part + wide[n * 8 : n * 8 + 8]
    weight_part = jnp.dot(
        jnp.transpose(agg.astype(f32)).astype(bf16), slope, preferred_element_type=f32
    )
    w_sem1, w_sem2, w_sem3, w_sem4, w_sem5, w_sem6 = (take(n) for n in (1, 3, 3, 3, 6, 1))
    for n in range(2):
        w1[n, 0:64] = weight_part[n * 64 : n * 64 + 64]
        w1[n, 64:72] = bias_part
    w_got1 = send(w1.at[1 - core], w1.at[2], w_sem1, dcore=1)
    out_ref[...] = (pre * sigma).astype(bf16)

    def in_order(me, own, received):
        total = None
        for n in range(4):
            term = own
            for d in (1, 2, 3):
                term = jnp.where(lax.rem(me + 4 - d, 4) == n, received[d - 1], term)
            total = term if total is None else total + term
        return total

    w_got1.wait_recv()
    pair = w1[core] + w1[2]
    for n in range(4):
        w2[n, 0:16] = pair[n * 16 : n * 16 + 16]
        w2[n, 16:24] = pair[64:72]
    w_got2 = [
        send(w2.at[lax.rem(y + d, 4)], w2.at[3 + d], w_sem2 + d - 1, dy=d) for d in (1, 2, 3)
    ]

    af, bf = {}, {}
    for e in near_first:
        ax[e].wait_recv()
        bz[e].wait_recv()

    def forward_to(d):
        for e in near_first:
            from_x = grads.at[lax.rem(x + 4 - e, 4) * 4 + z, 0]
            from_z = grads.at[x * 4 + lax.rem(z + 4 - e, 4), 1]
            af[e, d] = send(from_x, from_x, sem_af + (e - 1) * 3 + d - 1, dz=d)
            bf[e, d] = send(from_z, from_z, sem_bf + (e - 1) * 3 + d - 1, dx=d)

    forward_to(1)
    forward_to(3)

    for copy in w_got2:
        copy.wait_recv()
    w3[0] = in_order(y, w2[y], [w2[3 + d] for d in (1, 2, 3)])
    w_got3 = [send(w3.at[0], w3.at[d], w_sem3 + d - 1, dx=d) for d in (1, 2, 3)]
    forward_to(2)

    def group(g):
        zg, xg_ = lax.rem(z + 4 - g, 4), lax.rem(x + 4 - g, 4)
        return [(xx * 4 + zg, 0) for xx in range(4)] + [(xg_ * 4 + zz, 1) for zz in range(4)]

    def backward(g, i):
        members = group(g)
        lhs = jnp.concatenate([grads[j, h] for j, h in members], axis=1)
        rhs = jnp.concatenate(
            [
                jnp.concatenate([tile(2 * j + h, 2 * i + b) for b in range(2)], axis=1)
                for j, h in members
            ],
            axis=0,
        )
        return jnp.dot(lhs, rhs, preferred_element_type=f32)

    WIDE = 4

    def run_group(g, fresh):
        def some(m, carry):
            for u in range(WIDE):
                i = m * WIDE + u
                back[i] = backward(g, i) if fresh else back[i] + backward(g, i)
            return carry

        lax.fori_loop(0, 8 // WIDE, some, 0)

    def arrive(g):
        az[g].wait_recv()
        bx[g].wait_recv()
        for e in (1, 2, 3):
            af[e, g].wait_recv()
            bf[e, g].wait_recv()

    run_group(0, True)
    arrive(1)

    run_group(1, False)

    for copy in w_got3:
        copy.wait_recv()
    w4[0] = in_order(x, w3[0], [w3[d] for d in (1, 2, 3)])
    w_got4 = [send(w4.at[0], w4.at[d], w_sem4 + d - 1, dz=d) for d in (1, 2, 3)]

    arrive(3)
    run_group(3, False)

    arrive(2)
    rs_sem1, rs_sem2 = take(4), take(3)
    order = (2, 1, 3, 0)
    got1 = []
    for n, d in enumerate(order):
        r = lax.rem(y + d, 4) * 2 + (1 - core)
        rs1_out[n] = (back[r] + backward(2, r)).astype(bf16)
        got1.append(send(rs1_out.at[n], rs1_in.at[n], rs_sem1 + n, dcore=1))
    for copy in w_got4:
        copy.wait_recv()
    summed = in_order(z, w4[0], [w4[d] for d in (1, 2, 3)])
    scale = 1.0 / math.sqrt(256 * lax.axis_size("row") * lax.axis_size("col"))
    w5[core, y] = summed[0:16] * scale
    mine = w5.at[core, y]
    w_got5 = [send(mine, mine, w_sem6, dcore=1)]
    for d in (1, 2, 3):
        for other in range(2):
            w_got5.append(send(mine, mine, w_sem5 + 2 * d - 2 + other, dy=d, dcore=other))
    bgrad_ref[...] = jnp.sum(summed[16:24], axis=0, keepdims=True) * scale

    got2 = []
    own = []
    for d in order:
        r = lax.rem(y + d, 4) * 2 + core
        own.append(back[r] + backward(2, r))
    for n, d in enumerate(order):
        got1[n].wait_recv()
        total = own[n] + rs1_in[n].astype(f32)
        if d:
            rs2_out[n] = total.astype(bf16)
            got2.append(send(rs2_out.at[n], rs2_in.at[n], rs_sem2 + n, dy=d))

    for n in range(3):
        got2[n].wait_recv()
        total = total + rs2_in[n].astype(f32)
    fgrad_ref[...] = jnp.transpose(total)
    for copy in w_got5:
        copy.wait_recv()
    wgrad_ref[...] = w5[...].reshape(128, 256)
    for copy in sent:
        copy.wait_send()
    assert counter[0] <= SEMS, counter[0]


SEMS = 112


def local(features, tile_values, tile_coords, tile_count, weight, bias, cotangent):
    tiles = tile_values.shape[2]
    vmem = pl.BlockSpec(memory_space=pltpu.VMEM)
    anywhere = pl.BlockSpec(memory_space=pl.ANY)
    square = (BLK, BLK)
    out, wgrad, bgrad, fgrad = pl.pallas_call(
        kernel,
        name="graph_layer",
        out_shape=(
            pltpu.VMEM((256, 256), bf16),
            pltpu.VMEM((128, 256), f32),
            pltpu.VMEM((1, 256), f32),
            pltpu.VMEM((256, 128), f32),
        ),
        in_specs=[pl.BlockSpec(memory_space=pltpu.HBM)] * 7,
        out_specs=(vmem, vmem, vmem, vmem),
        scratch_shapes=[
            pltpu.VMEM((tiles // 2, *square), bf16),
            pltpu.VMEM((tiles // 2, *square), bf16),
            pltpu.VMEM((tiles + 1, *square), bf16),
            pltpu.VMEM((tiles // 2 + 1, *square), bf16),
            pltpu.VMEM((8, 256, 128), bf16),
            pltpu.VMEM((2, tiles), i32),
            pltpu.VMEM((1, 1), i32),
            pltpu.VMEM((128, 256), bf16),
            pltpu.VMEM((1, 256), f32),
            pltpu.VMEM((256, 256), bf16),
            pltpu.VMEM((2, tiles), i32),
            pltpu.SMEM((2, tiles), i32),
            pltpu.VMEM((4, 2, 4, *square), bf16),
            pltpu.VMEM((3, 4, *square), bf16),
            pltpu.VMEM((3, 4, *square), bf16),
            pltpu.VMEM((3, *square), bf16),
            pltpu.VMEM((3, *square), bf16),
            pltpu.VMEM((3, *square), bf16),
            pltpu.VMEM((3, *square), bf16),
            pltpu.VMEM((16, 2, *square), bf16),
            pltpu.VMEM((8, 128, 256), f32),
            pltpu.VMEM((4, 128, 256), bf16),
            pltpu.VMEM((4, 128, 256), bf16),
            pltpu.VMEM((3, 128, 256), bf16),
            pltpu.VMEM((3, 128, 256), bf16),
            pltpu.VMEM((3, 72, 256), f32),
            pltpu.VMEM((7, 24, 256), f32),
            pltpu.VMEM((4, 24, 256), f32),
            pltpu.VMEM((4, 24, 256), f32),
            pltpu.VMEM((2, 4, 16, 256), f32),
            pltpu.SemaphoreType.DMA((8,)),
            pltpu.SemaphoreType.DMA((SEMS,)),
            pltpu.SemaphoreType.DMA((SEMS,)),
        ],
        compiler_params=pltpu.CompilerParams(
            collective_id=0, has_side_effects=True, vmem_limit_bytes=56 * 2**20
        ),
    )(features, tile_values, tile_coords, tile_count, weight, bias.reshape(1, 256), cotangent)
    kinds = (((256, 256), bf16), ((128, 256), f32), ((1, 256), f32), ((256, 128), f32))
    out, wgrad, bgrad, fgrad = pl.pallas_call(
        finish,
        name="finish",
        out_shape=[jax.ShapeDtypeStruct(*kind) for kind in kinds],
        in_specs=[anywhere] * 4,
        out_specs=[anywhere] * 4,
        scratch_shapes=[pltpu.SemaphoreType.DMA((4,))],
    )(*(pltpu.with_memory_space_constraint(v, pltpu.VMEM) for v in (out, wgrad, bgrad, fgrad)))
    return out, wgrad, bgrad.reshape(256), fgrad


def finish(*refs):
    sems = refs[-1]
    copies = [pltpu.make_async_copy(refs[n], refs[4 + n], sems.at[n]) for n in range(4)]
    for copy in copies:
        copy.start()
    for copy in copies:
        copy.wait()


def solution(mesh):
    placed = (
        P(("row", "col"), None),
        P("row", "col", None, None, None),
        P("row", "col", None, None),
        P("row", "col"),
        P(),
        P(),
        P(("row", "col"), None),
    )
    return jax.shard_map(
        local,
        mesh=mesh,
        in_specs=placed,
        out_specs=(P(("row", "col"), None), P(), P(), P(("row", "col"), None)),
        check_vma=False,
    )
```
